32 devices in a mesh: parts: 2 (over x), sta: 16 (over z, y, core).
Axes of the slice: x: 2, y: 2, z: 4, core: 2. Of those that a mesh axis runs over, the one named last changes fastest.
Arguments:
- data: bfloat16 [32, 3, 896], P(('parts', 'sta')), parts along dimension 0, may hold values from -40 to 40
- templates: bfloat16 [128, 3, 512], P('sta'), may hold values from -12 to 12
- station_lists: int32 [16, 128], replicated, may hold values from 0 to 15, as said below
- counts: int32 [128], replicated, may hold values from 8 to 16
- offsets: int32 [16, 128], replicated, may hold values from 0 to 127
Outputs:
- detection: float32 [256, 256], P(('parts', 'sta')), parts along dimension 0
The draws below stay inside these ranges and needn't reach their ends.
There are 2 independent parts, one for each index of `parts`. The reference program is written for one: setup_inputs(seed, part) draws one part's arguments, and reference() takes and returns one part's arrays. A program takes and returns all parts, laid end to end along the dimension named above; an argument that names none is the same for every part. Nothing has to cross between parts.
Inputs may be any that keep to these rules, and one draw needn't show every extreme that they name: `station_lists`: each column names every one of the 16 stations once; template t uses the stations in entries k < counts[t] of its column. offsets[k, t] belongs to the station in entry k of template t's column.
All inputs are finite; a program needn't handle non-finite values.
Results may differ from the reference program's by a relative error of at most 0.0028.
Values may be sent and summed in bfloat16 or wider, within the bound.
A program may use at most 64 MiB of HBM per device.

```python
import math
import jax
import jax.numpy as jnp
from jax import lax

NCH = 3
L = 512
OFFMAX = 128
NTAU = 256
NSTA = 16
NT = 128
NS = 896


def draw_data(key, part):
    key_list = jax.random.split(key, 2)
    noise_part = jnp.clip(jax.random.normal(key_list[0], (NSTA, NCH, NS), jnp.float32), -4.0, 4.0)
    levels = jax.random.uniform(key_list[1], (NSTA, NCH, NS // 64, 1), jnp.float32, 0.0, math.log(10.0))
    envelope = jnp.broadcast_to(jnp.exp(levels), (NSTA, NCH, NS // 64, 64)).reshape(NSTA, NCH, NS)
    return (noise_part * envelope).astype(jnp.bfloat16)


def draw_templates(key, part):
    key_list = jax.random.split(key, 2)
    levels = jax.random.uniform(key_list[1], (NT, NCH, 1), jnp.float32, math.log(0.3), math.log(3.0))
    wave_part = jnp.clip(jax.random.normal(key_list[0], (NT, NCH, L), jnp.float32), -4.0, 4.0)
    return (wave_part * jnp.exp(levels)).astype(jnp.bfloat16)


def draw_station_lists(key, part):
    key_list = jax.random.split(jax.random.fold_in(key, 17), NT)
    columns = jax.vmap(lambda sub_key: jax.random.permutation(sub_key, NSTA))(key_list)
    return columns.T.astype(jnp.int32)


def draw_counts(key, part):
    key_list = jax.random.split(key, 3)
    values = jax.random.randint(key_list[0], (NT,), NSTA // 2, NSTA + 1, dtype=jnp.int32)
    top_slot = jax.random.randint(key_list[1], (), 0, NT, dtype=jnp.int32)
    low_slot = (top_slot + 1 + jax.random.randint(key_list[2], (), 0, NT - 1, dtype=jnp.int32)) % NT
    return values.at[top_slot].set(NSTA).at[low_slot].set(NSTA // 2)


def place_ends(values, key, low, top_value):
    place = [jax.random.randint(jax.random.fold_in(key, axis), (), 0, length) for axis, length in enumerate(values.shape)]
    longest = values.shape.index(max(values.shape))
    next_to = place[:longest] + [(place[longest] + 1) % values.shape[longest]] + place[longest + 1:]
    return values.at[tuple(place)].set(low).at[tuple(next_to)].set(top_value)


def setup_inputs(seed: int = 0, part: int = 0) -> dict:
    streams_of = jax.random.split(jax.random.key(seed), 6)
    part_splits = jax.random.split(jax.random.fold_in(streams_of[5], part), 6)
    return {
        "data": draw_data(jax.random.fold_in(jax.random.fold_in(streams_of[5], part), 71), part),
        "templates": draw_templates(jax.random.fold_in(streams_of[5], 71), part),
        "station_lists": draw_station_lists(jax.random.fold_in(streams_of[5], 71), part),
        "counts": draw_counts(jax.random.fold_in(streams_of[5], 71), part),
        "offsets": place_ends(jax.random.randint(streams_of[4], (NSTA, NT), 0, OFFMAX), jax.random.fold_in(streams_of[4], 1), 0, OFFMAX - 1).astype(jnp.int32),
    }


def reference(data, templates, station_lists, counts, offsets):
    lag_count = NTAU + OFFMAX
    lists_rows = station_lists.T
    offset_rows = offsets.T
    values = templates.astype(jnp.float32)
    centered = (values - lax.optimization_barrier(jnp.mean(values, axis=2, keepdims=True))).astype(jnp.bfloat16)
    cen_values = centered.astype(jnp.float32)
    chan_norms = jnp.sqrt(lax.optimization_barrier(jnp.mean(cen_values * cen_values, axis=2)) + 1e-06)
    samples = data.astype(jnp.float32)
    window_sum = lax.reduce_window(samples, 0.0, lax.add, (1, 1, L), (1, 1, 1), 'VALID')[:, :, :lag_count]
    square_sum = lax.reduce_window(samples * samples, 0.0, lax.add, (1, 1, L), (1, 1, 1), 'VALID')[:, :, :lag_count]
    mean_one = window_sum / L
    mean_two = square_sum / L
    scales = jnp.sqrt(mean_two - mean_one * mean_one + 1e-05)
    row_index = jnp.arange(NT, dtype=jnp.int32)[:, None]
    in_count = jnp.arange(NSTA, dtype=jnp.int32)[None, :] < counts[:, None]
    member = jnp.zeros((NT, NSTA), jnp.float32).at[row_index, lists_rows].set(in_count.astype(jnp.float32))
    shift_table = jnp.zeros((NT, NSTA), jnp.int32).at[row_index, lists_rows].set(jnp.where(in_count, offset_rows, 0).astype(jnp.int32))
    hankel_index = jnp.arange(lag_count, dtype=jnp.int32)[:, None] + jnp.arange(L, dtype=jnp.int32)[None, :]
    lag_index = jnp.arange(NTAU, dtype=jnp.int32)[None, :]

    def station_step(running, inputs):
        station_samples, station_scales, station_member, station_shift = inputs
        hankel = station_samples[:, hankel_index].astype(jnp.float32)
        products = jnp.einsum('tck,cuk->tcu', cen_values, hankel)
        normalized = products / (L * chan_norms[:, :, None] * station_scales[None])
        fitted = lax.optimization_barrier(jnp.mean(normalized, axis=1))
        picked = jnp.take_along_axis(fitted, lag_index + station_shift[:, None], axis=1)
        return (running + station_member[:, None] * picked, None)
    zero_rows = jnp.zeros((NT, NTAU), jnp.float32)
    stacked, _ = lax.scan(station_step, zero_rows, (data, scales, member.T, shift_table.T))
    return stacked
```

```python
import functools

import jax
import jax.numpy as jnp
from jax import lax
from jax.experimental import pallas as pl
from jax.experimental.pallas import tpu as pltpu
from jax.sharding import PartitionSpec as P

NCH = 3
L = 512
NTAU = 256
LANES = 128
SLOT = 24
F32 = jnp.float32
MESH = pl.DeviceIdType.MESH


def dot_nt(a, b):
    return lax.dot_general(a, b, (((1,), (1,)), ((), ())), preferred_element_type=F32)


def network_kernel(
    n, data_ref, templates_ref, lists_ref, counts_ref, offsets_ref, out_ref,
    slots, bands, send_sem, recv_sem,
):
    me = lax.axis_index("sta")
    samples_len = data_ref.shape[2]
    blocks = samples_len // LANES
    lag_blocks = (samples_len - L) // LANES
    out_blocks = NTAU // LANES
    wave_blocks = L // LANES
    span = L + LANES
    own = templates_ref.shape[1]

    barrier = pltpu.get_barrier_semaphore()

    @pl.loop(1, n)
    def greet(step):
        pl.semaphore_signal(
            barrier, inc=1, device_id={"sta": lax.rem(me + step, n)}, device_id_type=MESH
        )

    first_row = pl.multiple_of(me * SLOT, 8)
    own_samples = data_ref[0].astype(F32)
    rows = [own_samples[:, LANES * b : LANES * (b + 1)] for b in range(blocks)]
    rows.append(jnp.zeros((SLOT - NCH * blocks, LANES), F32))
    slots[pl.ds(first_row, SLOT), :] = jnp.concatenate(rows, axis=0)

    pl.semaphore_wait(barrier, n - 1)

    def copy_to(step):
        peer = lax.rem(me + step, n)
        return pltpu.make_async_remote_copy(
            src_ref=slots.at[pl.ds(first_row, SLOT), :],
            dst_ref=slots.at[pl.ds(first_row, SLOT), :],
            send_sem=send_sem.at[step],
            recv_sem=recv_sem.at[step],
            device_id={"sta": peer},
            device_id_type=MESH,
        )

    @pl.loop(1, n)
    def send(step):
        copy_to(step).start()

    row_id = lax.broadcasted_iota(jnp.int32, (LANES, LANES), 0)
    lane_id = lax.broadcasted_iota(jnp.int32, (LANES, LANES), 1)
    upper = lane_id >= row_id
    zeros = jnp.zeros((LANES, LANES), F32)
    factors = []
    for c in range(NCH):
        values = templates_ref[c].astype(F32)
        mean = jnp.sum(values, axis=1, keepdims=True) / L
        centered = (values - mean).astype(jnp.bfloat16).astype(F32)
        power = jnp.sum(centered * centered, axis=1, keepdims=True) / L
        factors.append(1.0 / (NCH * L * jnp.sqrt(power + 1e-06)))
        for t in range(own):
            before = zeros
            for k in range(wave_blocks + 1):
                if k < wave_blocks:
                    row = centered[t : t + 1, LANES * k : LANES * (k + 1)]
                    turned = pltpu.roll(
                        jnp.broadcast_to(row, (LANES, LANES)), 0, 1, stride=1, stride_axis=0
                    )
                else:
                    turned = zeros
                bands[c, LANES * t : LANES * (t + 1), LANES * k : LANES * (k + 1)] = jnp.where(
                    upper, turned, before
                ).astype(jnp.bfloat16)
                before = turned

    width = counts_ref.shape[1]
    station = lax.broadcasted_iota(jnp.int32, (n, width), 0)
    lane = lax.broadcasted_iota(jnp.int32, (n, width), 1)
    counts = counts_ref[...]
    table = jnp.zeros((n, width), jnp.int32)
    for k in range(lists_ref.shape[0]):
        match = (lists_ref[k : k + 1, :] == station) & (k < counts)
        table = table + jnp.where(match, offsets_ref[k : k + 1, :] + 256, 0)
    table = table.astype(F32)
    codes = [
        jnp.sum(jnp.where(lane == me * own + t, table, 0.0), axis=1, keepdims=True).astype(jnp.int32)
        for t in range(own)
    ]

    window_row = lax.broadcasted_iota(jnp.int32, (span, LANES), 0)
    window_lane = lax.broadcasted_iota(jnp.int32, (span, LANES), 1)
    window = ((window_row >= window_lane) & (window_row < window_lane + L)).astype(F32)
    window = window.astype(jnp.bfloat16)

    @pl.loop(1, n)
    def receive(step):
        sender = lax.rem(me - step + n, n)
        landed = slots.at[pl.ds(pl.multiple_of(sender * SLOT, 8), SLOT), :]
        pltpu.make_async_remote_copy(
            src_ref=landed,
            dst_ref=landed,
            send_sem=send_sem.at[step],
            recv_sem=recv_sem.at[step],
            device_id={"sta": sender},
            device_id_type=MESH,
        ).wait_recv()

    def spread(parts):
        return jnp.concatenate(
            [
                jnp.concatenate(parts[b : b + wave_blocks + 1], axis=1)
                for b in range(lag_blocks)
            ],
            axis=0,
        )

    held = lag_blocks * n
    operands, squares = [], []
    for c in range(NCH):
        parts = [slots[pl.ds(NCH * b + c, n, stride=SLOT), :] for b in range(blocks)]
        operands.append(spread([x.astype(jnp.bfloat16) for x in parts]))
        high = [(x * x).astype(jnp.bfloat16) for x in parts]
        low = [(x * x - h.astype(F32)).astype(jnp.bfloat16) for x, h in zip(parts, high)]
        squares.append((spread(high), spread(low)))
    fitted = [None] * own
    for c in range(NCH):
        stacked = jnp.concatenate([operands[c], *squares[c]], axis=0)
        sums = jnp.dot(stacked, window, preferred_element_type=F32)
        mean_one = sums[:held] / L
        mean_two = (sums[held : 2 * held] + sums[2 * held :]) / L
        inverse = 1.0 / jnp.sqrt(mean_two - mean_one * mean_one + 1e-05)
        products = dot_nt(operands[c], bands[c])
        for t in range(own):
            term = products[:, LANES * t : LANES * (t + 1)] * (inverse * factors[c][t : t + 1, :])
            fitted[t] = term if c == 0 else fitted[t] + term

    lane = lax.broadcasted_iota(jnp.int32, (n, LANES), 1)
    for t in range(own):
        code = jnp.broadcast_to(codes[t], (n, LANES))
        shift = code & 127
        member = code >= 256
        tiled = jnp.concatenate([shift] * lag_blocks, axis=0)
        current = fitted[t]
        for bit in range(7):
            step = 1 << bit
            current = jnp.where(
                (tiled & step) != 0, pltpu.roll(current, LANES - step, 1), current
            )
        stays = lane + shift < LANES
        for b in range(out_blocks):
            picked = jnp.where(
                stays, current[n * b : n * (b + 1)], current[n * (b + 1) : n * (b + 2)]
            )
            out_ref[t : t + 1, LANES * b : LANES * (b + 1)] = jnp.sum(
                jnp.where(member, picked, 0.0), axis=0, keepdims=True
            )

    @pl.loop(1, n)
    def sent(step):
        copy_to(step).wait_send()


def body(n, data, templates, station_lists, counts, offsets):
    own, _, length = templates.shape
    return pl.pallas_call(
        functools.partial(network_kernel, n),
        out_shape=jax.ShapeDtypeStruct((own, NTAU), F32),
        in_specs=[pl.BlockSpec(memory_space=pltpu.VMEM)] * 5,
        out_specs=pl.BlockSpec(memory_space=pltpu.VMEM),
        scratch_shapes=[
            pltpu.VMEM((n * SLOT, LANES), F32),
            pltpu.VMEM((NCH, own * LANES, length + LANES), jnp.bfloat16),
            pltpu.SemaphoreType.DMA((n,)),
            pltpu.SemaphoreType.DMA((n,)),
        ],
        compiler_params=pltpu.CompilerParams(
            collective_id=0, has_side_effects=True, vmem_limit_bytes=40 * 1024 * 1024
        ),
    )(data, jnp.transpose(templates, (1, 0, 2)), station_lists, counts[None, :], offsets)


def solution(mesh):
    placed = (P(("parts", "sta"), None, None), P("sta", None, None), P(), P(), P())
    return jax.shard_map(
        functools.partial(body, mesh.shape["sta"]), mesh=mesh, in_specs=placed,
        out_specs=P(("parts", "sta"), None), check_vma=False,
    )
```

```python
import functools

import jax
import jax.numpy as jnp
from jax import lax
from jax.experimental import pallas as pl
from jax.experimental.pallas import tpu as pltpu
from jax.sharding import PartitionSpec as P

NCH = 3
L = 512
NTAU = 256
LANES = 128
SLOT = 24
F32 = jnp.float32
MESH = pl.DeviceIdType.MESH


def dot_nt(a, b):
    return lax.dot_general(a, b, (((1,), (1,)), ((), ())), preferred_element_type=F32)


def network_kernel(
    n, data_hbm, templates_hbm, lists_hbm, counts_hbm, offsets_hbm, out_ref,
    data_ref, templates_ref, lists_ref, counts_ref, offsets_ref,
    slots, bands, fetch_sem, send_sem, recv_sem,
):
    fetches = [
        pltpu.make_async_copy(source, target, fetch_sem.at[i])
        for i, (source, target) in enumerate(
            [
                (data_hbm, data_ref), (templates_hbm, templates_ref), (lists_hbm, lists_ref),
                (counts_hbm, counts_ref), (offsets_hbm, offsets_ref),
            ]
        )
    ]
    for fetch in fetches:
        fetch.start()
    me = lax.axis_index("sta")
    samples_len = data_ref.shape[2]
    blocks = samples_len // LANES
    lag_blocks = (samples_len - L) // LANES
    out_blocks = NTAU // LANES
    wave_blocks = L // LANES
    span = L + LANES
    own = templates_ref.shape[1]

    barrier = pltpu.get_barrier_semaphore()

    @pl.loop(1, n)
    def greet(step):
        pl.semaphore_signal(
            barrier, inc=1, device_id={"sta": lax.rem(me + step, n)}, device_id_type=MESH
        )

    first_row = pl.multiple_of(me * SLOT, 8)
    fetches[0].wait()
    own_samples = data_ref[0].astype(F32)
    rows = [own_samples[:, LANES * b : LANES * (b + 1)] for b in range(blocks)]
    rows.append(jnp.zeros((SLOT - NCH * blocks, LANES), F32))
    slots[pl.ds(first_row, SLOT), :] = jnp.concatenate(rows, axis=0)

    pl.semaphore_wait(barrier, n - 1)

    def copy_to(step):
        peer = lax.rem(me + step, n)
        return pltpu.make_async_remote_copy(
            src_ref=slots.at[pl.ds(first_row, SLOT), :],
            dst_ref=slots.at[pl.ds(first_row, SLOT), :],
            send_sem=send_sem.at[step],
            recv_sem=recv_sem.at[step],
            device_id={"sta": peer},
            device_id_type=MESH,
        )

    @pl.loop(1, n)
    def send(step):
        copy_to(step).start()

    row_id = lax.broadcasted_iota(jnp.int32, (LANES, LANES), 0)
    lane_id = lax.broadcasted_iota(jnp.int32, (LANES, LANES), 1)
    upper = lane_id >= row_id
    zeros = jnp.zeros((LANES, LANES), F32)
    factors = []
    fetches[1].wait()
    for c in range(NCH):
        values = templates_ref[c].astype(F32)
        mean = jnp.sum(values, axis=1, keepdims=True) / L
        centered = (values - mean).astype(jnp.bfloat16).astype(F32)
        power = jnp.sum(centered * centered, axis=1, keepdims=True) / L
        factors.append(1.0 / (NCH * L * jnp.sqrt(power + 1e-06)))
        for t in range(own):
            before = zeros
            for k in range(wave_blocks + 1):
                if k < wave_blocks:
                    row = centered[t : t + 1, LANES * k : LANES * (k + 1)]
                    turned = pltpu.roll(
                        jnp.broadcast_to(row, (LANES, LANES)), 0, 1, stride=1, stride_axis=0
                    )
                else:
                    turned = zeros
                bands[c, LANES * t : LANES * (t + 1), LANES * k : LANES * (k + 1)] = jnp.where(
                    upper, turned, before
                ).astype(jnp.bfloat16)
                before = turned

    for fetch in fetches[2:]:
        fetch.wait()
    width = counts_ref.shape[1]
    station = lax.broadcasted_iota(jnp.int32, (n, width), 0)
    lane = lax.broadcasted_iota(jnp.int32, (n, width), 1)
    counts = counts_ref[...]
    table = jnp.zeros((n, width), jnp.int32)
    for k in range(lists_ref.shape[0]):
        match = (lists_ref[k : k + 1, :] == station) & (k < counts)
        table = table + jnp.where(match, offsets_ref[k : k + 1, :] + 256, 0)
    table = table.astype(F32)
    codes = [
        jnp.sum(jnp.where(lane == me * own + t, table, 0.0), axis=1, keepdims=True).astype(jnp.int32)
        for t in range(own)
    ]

    window_row = lax.broadcasted_iota(jnp.int32, (span, LANES), 0)
    window_lane = lax.broadcasted_iota(jnp.int32, (span, LANES), 1)
    window = ((window_row >= window_lane) & (window_row < window_lane + L)).astype(F32)
    window = window.astype(jnp.bfloat16)

    @pl.loop(1, n)
    def receive(step):
        sender = lax.rem(me - step + n, n)
        landed = slots.at[pl.ds(pl.multiple_of(sender * SLOT, 8), SLOT), :]
        pltpu.make_async_remote_copy(
            src_ref=landed,
            dst_ref=landed,
            send_sem=send_sem.at[step],
            recv_sem=recv_sem.at[step],
            device_id={"sta": sender},
            device_id_type=MESH,
        ).wait_recv()

    def spread(parts):
        return jnp.concatenate(
            [
                jnp.concatenate(parts[b : b + wave_blocks + 1], axis=1)
                for b in range(lag_blocks)
            ],
            axis=0,
        )

    held = lag_blocks * n
    operands, squares = [], []
    for c in range(NCH):
        parts = [slots[pl.ds(NCH * b + c, n, stride=SLOT), :] for b in range(blocks)]
        operands.append(spread([x.astype(jnp.bfloat16) for x in parts]))
        high = [(x * x).astype(jnp.bfloat16) for x in parts]
        low = [(x * x - h.astype(F32)).astype(jnp.bfloat16) for x, h in zip(parts, high)]
        squares.append((spread(high), spread(low)))
    fitted = [None] * own
    for c in range(NCH):
        stacked = jnp.concatenate([operands[c], *squares[c]], axis=0)
        sums = jnp.dot(stacked, window, preferred_element_type=F32)
        mean_one = sums[:held] / L
        mean_two = (sums[held : 2 * held] + sums[2 * held :]) / L
        inverse = 1.0 / jnp.sqrt(mean_two - mean_one * mean_one + 1e-05)
        products = dot_nt(operands[c], bands[c])
        for t in range(own):
            term = products[:, LANES * t : LANES * (t + 1)] * (inverse * factors[c][t : t + 1, :])
            fitted[t] = term if c == 0 else fitted[t] + term

    lane = lax.broadcasted_iota(jnp.int32, (n, LANES), 1)
    for t in range(own):
        code = jnp.broadcast_to(codes[t], (n, LANES))
        shift = code & 127
        member = code >= 256
        tiled = jnp.concatenate([shift] * lag_blocks, axis=0)
        current = fitted[t]
        for bit in range(7):
            step = 1 << bit
            current = jnp.where(
                (tiled & step) != 0, pltpu.roll(current, LANES - step, 1), current
            )
        stays = lane + shift < LANES
        for b in range(out_blocks):
            picked = jnp.where(
                stays, current[n * b : n * (b + 1)], current[n * (b + 1) : n * (b + 2)]
            )
            out_ref[t : t + 1, LANES * b : LANES * (b + 1)] = jnp.sum(
                jnp.where(member, picked, 0.0), axis=0, keepdims=True
            )

    @pl.loop(1, n)
    def sent(step):
        copy_to(step).wait_send()


def body(n, data, templates, station_lists, counts, offsets):
    own, _, length = templates.shape
    operands = (data, jnp.transpose(templates, (1, 0, 2)), station_lists, counts[None, :], offsets)
    return pl.pallas_call(
        functools.partial(network_kernel, n),
        out_shape=jax.ShapeDtypeStruct((own, NTAU), F32),
        in_specs=[pl.BlockSpec(memory_space=pltpu.HBM)] * len(operands),
        out_specs=pl.BlockSpec(memory_space=pltpu.VMEM),
        scratch_shapes=[pltpu.VMEM(x.shape, x.dtype) for x in operands]
        + [
            pltpu.VMEM((n * SLOT, LANES), F32),
            pltpu.VMEM((NCH, own * LANES, length + LANES), jnp.bfloat16),
            pltpu.SemaphoreType.DMA((len(operands),)),
            pltpu.SemaphoreType.DMA((n,)),
            pltpu.SemaphoreType.DMA((n,)),
        ],
        compiler_params=pltpu.CompilerParams(
            collective_id=0, has_side_effects=True, vmem_limit_bytes=40 * 1024 * 1024
        ),
    )(*[pltpu.with_memory_space_constraint(x, pltpu.HBM) for x in operands])


def solution(mesh):
    placed = (P(("parts", "sta"), None, None), P("sta", None, None), P(), P(), P())
    return jax.shard_map(
        functools.partial(body, mesh.shape["sta"]), mesh=mesh, in_specs=placed,
        out_specs=P(("parts", "sta"), None), check_vma=False,
    )
```

```python
import functools

import jax
import jax.numpy as jnp
from jax import lax
from jax.experimental import pallas as pl
from jax.experimental.pallas import tpu as pltpu
from jax.sharding import PartitionSpec as P

NCH = 3
L = 512
NTAU = 256
LANES = 128
ROWS = 8
F32 = jnp.float32
MESH = pl.DeviceIdType.MESH


def dot_nt(a, b):
    return lax.dot_general(a, b, (((1,), (1,)), ((), ())), preferred_element_type=F32)


def network_kernel(
    n, data_hbm, templates_hbm, lists_hbm, counts_hbm, offsets_hbm, out_ref,
    templates_ref, lists_ref, counts_ref, offsets_ref,
    slots, staged, bands, fetch_sem, send_sem, recv_sem,
):
    me = lax.axis_index("sta")
    fetches = [
        pltpu.make_async_copy(source, target, fetch_sem.at[i])
        for i, (source, target) in enumerate(
            [
                (data_hbm.at[0], slots.at[me]), (templates_hbm, templates_ref), (lists_hbm, lists_ref),
                (counts_hbm, counts_ref), (offsets_hbm, offsets_ref),
            ]
        )
    ]
    for fetch in fetches:
        fetch.start()
    samples_len = data_hbm.shape[2]
    blocks = samples_len // LANES
    lag_blocks = (samples_len - L) // LANES
    out_blocks = NTAU // LANES
    wave_blocks = L // LANES
    span = L + LANES
    own = templates_ref.shape[1]

    barrier = pltpu.get_barrier_semaphore()

    @pl.loop(1, n)
    def greet(step):
        pl.semaphore_signal(
            barrier, inc=1, device_id={"sta": lax.rem(me + step, n)}, device_id_type=MESH
        )

    pl.semaphore_wait(barrier, n - 1)

    def copy_to(step):
        return pltpu.make_async_remote_copy(
            src_ref=data_hbm.at[0],
            dst_ref=slots.at[me],
            send_sem=send_sem.at[step],
            recv_sem=recv_sem.at[step],
            device_id={"sta": lax.rem(me + step, n)},
            device_id_type=MESH,
        )

    @pl.loop(1, n)
    def send(step):
        copy_to(step).start()

    row_id = lax.broadcasted_iota(jnp.int32, (LANES, LANES), 0)
    lane_id = lax.broadcasted_iota(jnp.int32, (LANES, LANES), 1)
    upper = lane_id >= row_id
    zeros = jnp.zeros((LANES, LANES), F32)
    factors = []
    fetches[1].wait()
    for c in range(NCH):
        values = templates_ref[c].astype(F32)
        mean = jnp.sum(values, axis=1, keepdims=True) / L
        centered = (values - mean).astype(jnp.bfloat16).astype(F32)
        power = jnp.sum(centered * centered, axis=1, keepdims=True) / L
        factors.append(1.0 / (NCH * L * jnp.sqrt(power + 1e-06)))
        for t in range(own):
            before = zeros
            for k in range(wave_blocks + 1):
                if k < wave_blocks:
                    row = centered[t : t + 1, LANES * k : LANES * (k + 1)]
                    turned = pltpu.roll(
                        jnp.broadcast_to(row, (LANES, LANES)), 0, 1, stride=1, stride_axis=0
                    )
                else:
                    turned = zeros
                bands[c, LANES * t : LANES * (t + 1), LANES * k : LANES * (k + 1)] = jnp.where(
                    upper, turned, before
                ).astype(jnp.bfloat16)
                before = turned

    for fetch in fetches[2:]:
        fetch.wait()
    width = counts_ref.shape[1]
    station = lax.broadcasted_iota(jnp.int32, (n, width), 0)
    lane = lax.broadcasted_iota(jnp.int32, (n, width), 1)
    counts = counts_ref[...]
    table = jnp.zeros((n, width), jnp.int32)
    for k in range(lists_ref.shape[0]):
        match = (lists_ref[k : k + 1, :] == station) & (k < counts)
        table = table + jnp.where(match, offsets_ref[k : k + 1, :] + 256, 0)
    table = table.astype(F32)
    codes = [
        jnp.sum(jnp.where(lane == me * own + t, table, 0.0), axis=1, keepdims=True).astype(jnp.int32)
        for t in range(own)
    ]

    window_row = lax.broadcasted_iota(jnp.int32, (span, LANES), 0)
    window_lane = lax.broadcasted_iota(jnp.int32, (span, LANES), 1)
    window = ((window_row >= window_lane) & (window_row < window_lane + L)).astype(F32)
    window = window.astype(jnp.bfloat16)

    def stage(sender):
        samples = slots[sender].astype(F32)
        for b in range(blocks):
            first_row = pl.multiple_of(sender * (ROWS * blocks) + ROWS * b, ROWS)
            staged[pl.ds(first_row, NCH), :] = samples[:, LANES * b : LANES * (b + 1)]

    fetches[0].wait()
    stage(me)

    @pl.loop(1, n)
    def receive(step):
        sender = lax.rem(me - step + n, n)
        pltpu.make_async_remote_copy(
            src_ref=data_hbm.at[0],
            dst_ref=slots.at[sender],
            send_sem=send_sem.at[step],
            recv_sem=recv_sem.at[step],
            device_id={"sta": sender},
            device_id_type=MESH,
        ).wait_recv()
        stage(sender)

    def spread(parts):
        return jnp.concatenate(
            [
                jnp.concatenate(parts[b : b + wave_blocks + 1], axis=1)
                for b in range(lag_blocks)
            ],
            axis=0,
        )

    held = lag_blocks * n
    operands, squares = [], []
    for c in range(NCH):
        parts = [staged[pl.ds(ROWS * b + c, n, stride=ROWS * blocks), :] for b in range(blocks)]
        operands.append(spread([x.astype(jnp.bfloat16) for x in parts]))
        high = [(x * x).astype(jnp.bfloat16) for x in parts]
        low = [(x * x - h.astype(F32)).astype(jnp.bfloat16) for x, h in zip(parts, high)]
        squares.append((spread(high), spread(low)))
    fitted = [None] * own
    for c in range(NCH):
        stacked = jnp.concatenate([operands[c], *squares[c]], axis=0)
        sums = jnp.dot(stacked, window, preferred_element_type=F32)
        mean_one = sums[:held] / L
        mean_two = (sums[held : 2 * held] + sums[2 * held :]) / L
        inverse = 1.0 / jnp.sqrt(mean_two - mean_one * mean_one + 1e-05)
        products = dot_nt(operands[c], bands[c])
        for t in range(own):
            term = products[:, LANES * t : LANES * (t + 1)] * (inverse * factors[c][t : t + 1, :])
            fitted[t] = term if c == 0 else fitted[t] + term

    lane = lax.broadcasted_iota(jnp.int32, (n, LANES), 1)
    for t in range(own):
        code = jnp.broadcast_to(codes[t], (n, LANES))
        shift = code & 127
        member = code >= 256
        tiled = jnp.concatenate([shift] * lag_blocks, axis=0)
        current = fitted[t]
        for bit in range(7):
            step = 1 << bit
            current = jnp.where(
                (tiled & step) != 0, pltpu.roll(current, LANES - step, 1), current
            )
        stays = lane + shift < LANES
        for b in range(out_blocks):
            picked = jnp.where(
                stays, current[n * b : n * (b + 1)], current[n * (b + 1) : n * (b + 2)]
            )
            out_ref[t : t + 1, LANES * b : LANES * (b + 1)] = jnp.sum(
                jnp.where(member, picked, 0.0), axis=0, keepdims=True
            )

    @pl.loop(1, n)
    def sent(step):
        copy_to(step).wait_send()


def body(n, data, templates, station_lists, counts, offsets):
    own, _, length = templates.shape
    operands = (data, jnp.transpose(templates, (1, 0, 2)), station_lists, counts[None, :], offsets)
    return pl.pallas_call(
        functools.partial(network_kernel, n),
        out_shape=jax.ShapeDtypeStruct((own, NTAU), F32),
        in_specs=[pl.BlockSpec(memory_space=pltpu.HBM)] * len(operands),
        out_specs=pl.BlockSpec(memory_space=pltpu.VMEM),
        scratch_shapes=[pltpu.VMEM(x.shape, x.dtype) for x in operands[1:]]
        + [
            pltpu.VMEM((n, *data.shape[1:]), data.dtype),
            pltpu.VMEM((n * ROWS * (data.shape[2] // LANES), LANES), F32),
            pltpu.VMEM((NCH, own * LANES, length + LANES), jnp.bfloat16),
            pltpu.SemaphoreType.DMA((len(operands),)),
            pltpu.SemaphoreType.DMA((n,)),
            pltpu.SemaphoreType.DMA((n,)),
        ],
        compiler_params=pltpu.CompilerParams(
            collective_id=0, has_side_effects=True, vmem_limit_bytes=40 * 1024 * 1024
        ),
    )(*[pltpu.with_memory_space_constraint(x, pltpu.HBM) for x in operands])


def solution(mesh):
    placed = (P(("parts", "sta"), None, None), P("sta", None, None), P(), P(), P())
    return jax.shard_map(
        functools.partial(body, mesh.shape["sta"]), mesh=mesh, in_specs=placed,
        out_specs=P(("parts", "sta"), None), check_vma=False,
    )
```

```python
import functools

import jax
import jax.numpy as jnp
from jax import lax
from jax.experimental import pallas as pl
from jax.experimental.pallas import tpu as pltpu
from jax.sharding import PartitionSpec as P

NCH = 3
L = 512
NTAU = 256
LANES = 128
ROWS = 8
F32 = jnp.float32
MESH = pl.DeviceIdType.MESH


def dot_nt(a, b):
    return lax.dot_general(a, b, (((1,), (1,)), ((), ())), preferred_element_type=F32)


def network_kernel(
    n, data_hbm, templates_hbm, lists_hbm, counts_hbm, offsets_hbm, out_ref,
    templates_ref, lists_ref, counts_ref, offsets_ref,
    slots, staged, bands, fetch_sem, send_sem, recv_sem,
):
    me = lax.axis_index("sta")
    fetches = [
        pltpu.make_async_copy(source, target, fetch_sem.at[i])
        for i, (source, target) in enumerate(
            [
                (data_hbm.at[0], slots.at[me]), (templates_hbm, templates_ref), (lists_hbm, lists_ref),
                (counts_hbm, counts_ref), (offsets_hbm, offsets_ref),
            ]
        )
    ]
    fetches[0].start()
    samples_len = data_hbm.shape[2]
    blocks = samples_len // LANES
    lag_blocks = (samples_len - L) // LANES
    out_blocks = NTAU // LANES
    wave_blocks = L // LANES
    span = L + LANES
    own = templates_ref.shape[1]

    barrier = pltpu.get_barrier_semaphore()

    for step in range(1, n):
        pl.semaphore_signal(
            barrier, inc=1, device_id={"sta": lax.rem(me + step, n)}, device_id_type=MESH
        )

    pl.semaphore_wait(barrier, n - 1)

    def copy_to(step):
        return pltpu.make_async_remote_copy(
            src_ref=slots.at[me],
            dst_ref=slots.at[me],
            send_sem=send_sem.at[step],
            recv_sem=recv_sem.at[step],
            device_id={"sta": lax.rem(me + step, n)},
            device_id_type=MESH,
        )

    fetches[0].wait()
    for step in range(1, n):
        copy_to(step).start()
    for fetch in fetches[1:]:
        fetch.start()

    row_id = lax.broadcasted_iota(jnp.int32, (LANES, LANES), 0)
    lane_id = lax.broadcasted_iota(jnp.int32, (LANES, LANES), 1)
    upper = lane_id >= row_id
    zeros = jnp.zeros((LANES, LANES), F32)
    factors = []
    fetches[1].wait()
    for c in range(NCH):
        values = templates_ref[c].astype(F32)
        mean = jnp.sum(values, axis=1, keepdims=True) / L
        centered = (values - mean).astype(jnp.bfloat16).astype(F32)
        power = jnp.sum(centered * centered, axis=1, keepdims=True) / L
        factors.append(1.0 / (NCH * L * jnp.sqrt(power + 1e-06)))
        for t in range(own):
            before = zeros
            for k in range(wave_blocks + 1):
                if k < wave_blocks:
                    row = centered[t : t + 1, LANES * k : LANES * (k + 1)]
                    turned = pltpu.roll(
                        jnp.broadcast_to(row, (LANES, LANES)), 0, 1, stride=1, stride_axis=0
                    )
                else:
                    turned = zeros
                bands[c, LANES * t : LANES * (t + 1), LANES * k : LANES * (k + 1)] = jnp.where(
                    upper, turned, before
                ).astype(jnp.bfloat16)
                before = turned

    for fetch in fetches[2:]:
        fetch.wait()
    width = counts_ref.shape[1]
    station = lax.broadcasted_iota(jnp.int32, (n, width), 0)
    lane = lax.broadcasted_iota(jnp.int32, (n, width), 1)
    counts = counts_ref[...]
    table = jnp.zeros((n, width), jnp.int32)
    for k in range(lists_ref.shape[0]):
        match = (lists_ref[k : k + 1, :] == station) & (k < counts)
        table = table + jnp.where(match, offsets_ref[k : k + 1, :] + 256, 0)
    table = table.astype(F32)
    codes = [
        jnp.sum(jnp.where(lane == me * own + t, table, 0.0), axis=1, keepdims=True).astype(jnp.int32)
        for t in range(own)
    ]

    window_row = lax.broadcasted_iota(jnp.int32, (span, LANES), 0)
    window_lane = lax.broadcasted_iota(jnp.int32, (span, LANES), 1)
    window = ((window_row >= window_lane) & (window_row < window_lane + L)).astype(F32)
    window = window.astype(jnp.bfloat16)

    def stage(sender):
        samples = slots[sender].astype(F32)
        for b in range(blocks):
            first_row = pl.multiple_of(sender * (ROWS * blocks) + ROWS * b, ROWS)
            staged[pl.ds(first_row, NCH), :] = samples[:, LANES * b : LANES * (b + 1)]

    stage(me)

    @pl.loop(1, n)
    def receive(ahead):
        step = n - ahead
        sender = lax.rem(me + ahead, n)
        pltpu.make_async_remote_copy(
            src_ref=slots.at[sender],
            dst_ref=slots.at[sender],
            send_sem=send_sem.at[step],
            recv_sem=recv_sem.at[step],
            device_id={"sta": sender},
            device_id_type=MESH,
        ).wait_recv()
        stage(sender)

    def spread(parts):
        return jnp.concatenate(
            [
                jnp.concatenate(parts[b : b + wave_blocks + 1], axis=1)
                for b in range(lag_blocks)
            ],
            axis=0,
        )

    held = lag_blocks * n
    operands, squares = [], []
    for c in range(NCH):
        parts = [staged[pl.ds(ROWS * b + c, n, stride=ROWS * blocks), :] for b in range(blocks)]
        operands.append(spread([x.astype(jnp.bfloat16) for x in parts]))
        high = [(x * x).astype(jnp.bfloat16) for x in parts]
        low = [(x * x - h.astype(F32)).astype(jnp.bfloat16) for x, h in zip(parts, high)]
        squares.append((spread(high), spread(low)))
    fitted = [None] * own
    for c in range(NCH):
        stacked = jnp.concatenate([operands[c], *squares[c]], axis=0)
        sums = jnp.dot(stacked, window, preferred_element_type=F32)
        mean_one = sums[:held] / L
        mean_two = (sums[held : 2 * held] + sums[2 * held :]) / L
        inverse = 1.0 / jnp.sqrt(mean_two - mean_one * mean_one + 1e-05)
        products = dot_nt(operands[c], bands[c])
        for t in range(own):
            term = products[:, LANES * t : LANES * (t + 1)] * (inverse * factors[c][t : t + 1, :])
            fitted[t] = term if c == 0 else fitted[t] + term

    lane = lax.broadcasted_iota(jnp.int32, (n, LANES), 1)
    for t in range(own):
        code = jnp.broadcast_to(codes[t], (n, LANES))
        shift = code & 127
        member = code >= 256
        turn = (lane + shift) & (LANES - 1)
        current = jnp.take_along_axis(
            fitted[t], jnp.concatenate([turn] * lag_blocks, axis=0), axis=1,
            mode="promise_in_bounds",
        )
        stays = lane + shift < LANES
        for b in range(out_blocks):
            picked = jnp.where(
                stays, current[n * b : n * (b + 1)], current[n * (b + 1) : n * (b + 2)]
            )
            out_ref[t : t + 1, LANES * b : LANES * (b + 1)] = jnp.sum(
                jnp.where(member, picked, 0.0), axis=0, keepdims=True
            )

    @pl.loop(1, n)
    def sent(step):
        copy_to(step).wait_send()


def body(n, data, templates, station_lists, counts, offsets):
    own, _, length = templates.shape
    operands = (data, jnp.transpose(templates, (1, 0, 2)), station_lists, counts[None, :], offsets)
    return pl.pallas_call(
        functools.partial(network_kernel, n),
        out_shape=jax.ShapeDtypeStruct((own, NTAU), F32),
        in_specs=[pl.BlockSpec(memory_space=pltpu.HBM)] * len(operands),
        out_specs=pl.BlockSpec(memory_space=pltpu.VMEM),
        scratch_shapes=[pltpu.VMEM(x.shape, x.dtype) for x in operands[1:]]
        + [
            pltpu.VMEM((n, *data.shape[1:]), data.dtype),
            pltpu.VMEM((n * ROWS * (data.shape[2] // LANES), LANES), F32),
            pltpu.VMEM((NCH, own * LANES, length + LANES), jnp.bfloat16),
            pltpu.SemaphoreType.DMA((len(operands),)),
            pltpu.SemaphoreType.DMA((n,)),
            pltpu.SemaphoreType.DMA((n,)),
        ],
        compiler_params=pltpu.CompilerParams(
            collective_id=0, has_side_effects=True, vmem_limit_bytes=40 * 1024 * 1024
        ),
    )(*[pltpu.with_memory_space_constraint(x, pltpu.HBM) for x in operands])


def solution(mesh):
    placed = (P(("parts", "sta"), None, None), P("sta", None, None), P(), P(), P())
    return jax.shard_map(
        functools.partial(body, mesh.shape["sta"]), mesh=mesh, in_specs=placed,
        out_specs=P(("parts", "sta"), None), check_vma=False,
    )
```

```python
import functools

import jax
import jax.numpy as jnp
from jax import lax
from jax.experimental import pallas as pl
from jax.experimental.pallas import tpu as pltpu
from jax.sharding import PartitionSpec as P

NCH = 3
L = 512
NTAU = 256
LANES = 128
ROWS = 8
F32 = jnp.float32
MESH = pl.DeviceIdType.MESH


def network_kernel(
    n, data_hbm, templates_hbm, lists_hbm, counts_hbm, offsets_hbm, out_ref,
    templates_ref, lists_ref, counts_ref, offsets_ref,
    slots, staged, bands, factors_ref, fetch_sem, send_sem, recv_sem,
):
    me = lax.axis_index("sta")
    fetches = [
        pltpu.make_async_copy(source, target, fetch_sem.at[i])
        for i, (source, target) in enumerate(
            [
                (data_hbm.at[0], slots.at[me]), (templates_hbm, templates_ref), (lists_hbm, lists_ref),
                (counts_hbm, counts_ref), (offsets_hbm, offsets_ref),
            ]
        )
    ]
    fetches[0].start()
    fetches[1].start()
    samples_len = data_hbm.shape[2]
    blocks = samples_len // LANES
    lag_blocks = (samples_len - L) // LANES
    out_blocks = NTAU // LANES
    wave_blocks = L // LANES
    span = L + LANES
    own = templates_ref.shape[1]

    barrier = pltpu.get_barrier_semaphore()

    for step in range(1, n):
        pl.semaphore_signal(
            barrier, inc=1, device_id={"sta": lax.rem(me + step, n)}, device_id_type=MESH
        )

    row_id = lax.broadcasted_iota(jnp.int32, (LANES, LANES), 0)
    lane_id = lax.broadcasted_iota(jnp.int32, (LANES, LANES), 1)
    upper = lane_id >= row_id
    zeros = jnp.zeros((LANES, LANES), F32)

    def build():
        fetches[1].wait()
        for c in range(NCH):
            values = templates_ref[c].astype(F32)
            mean = jnp.sum(values, axis=1, keepdims=True) / L
            centered = (values - mean).astype(jnp.bfloat16).astype(F32)
            power = jnp.sum(centered * centered, axis=1, keepdims=True) / L
            factor = 1.0 / (NCH * L * jnp.sqrt(power + 1e-06))
            factors_ref[c] = jnp.broadcast_to(factor, (own, LANES))
            for t in range(own):
                before = zeros
                for k in range(wave_blocks + 1):
                    if k < wave_blocks:
                        row = centered[t : t + 1, LANES * k : LANES * (k + 1)]
                        turned = pltpu.roll(
                            jnp.broadcast_to(row, (LANES, LANES)), 0, 1, stride=1, stride_axis=0
                        )
                    else:
                        turned = zeros
                    bands[c, LANES * k : LANES * (k + 1), LANES * t : LANES * (t + 1)] = (
                        jnp.where(upper, turned, before).T.astype(jnp.bfloat16)
                    )
                    before = turned

    pl.when(me < n // 4)(build)

    pl.semaphore_wait(barrier, n - 1)

    def copy_to(step):
        return pltpu.make_async_remote_copy(
            src_ref=slots.at[me],
            dst_ref=slots.at[me],
            send_sem=send_sem.at[step],
            recv_sem=recv_sem.at[step],
            device_id={"sta": lax.rem(me + step, n)},
            device_id_type=MESH,
        )

    fetches[0].wait()
    for step in range(1, n):
        copy_to(step).start()
    for fetch in fetches[2:]:
        fetch.start()
    pl.when(me >= n // 4)(build)

    for fetch in fetches[2:]:
        fetch.wait()
    width = counts_ref.shape[1]
    station = lax.broadcasted_iota(jnp.int32, (n, width), 0)
    lane = lax.broadcasted_iota(jnp.int32, (n, width), 1)
    counts = counts_ref[...]
    table = jnp.zeros((n, width), jnp.int32)
    for k in range(lists_ref.shape[0]):
        match = (lists_ref[k : k + 1, :] == station) & (k < counts)
        table = table + jnp.where(match, offsets_ref[k : k + 1, :] + 256, 0)
    table = table.astype(F32)
    codes = [
        jnp.sum(jnp.where(lane == me * own + t, table, 0.0), axis=1, keepdims=True).astype(jnp.int32)
        for t in range(own)
    ]

    window_row = lax.broadcasted_iota(jnp.int32, (span, LANES), 0)
    window_lane = lax.broadcasted_iota(jnp.int32, (span, LANES), 1)
    window = ((window_row >= window_lane) & (window_row < window_lane + L)).astype(F32)
    window = window.astype(jnp.bfloat16)

    def stage(sender):
        samples = slots[sender].astype(F32)
        for b in range(blocks):
            first_row = pl.multiple_of(sender * (ROWS * blocks) + ROWS * b, ROWS)
            staged[pl.ds(first_row, NCH), :] = samples[:, LANES * b : LANES * (b + 1)]

    stage(me)

    @pl.loop(1, n)
    def receive(ahead):
        step = n - ahead
        sender = lax.rem(me + ahead, n)
        pltpu.make_async_remote_copy(
            src_ref=slots.at[sender],
            dst_ref=slots.at[sender],
            send_sem=send_sem.at[step],
            recv_sem=recv_sem.at[step],
            device_id={"sta": sender},
            device_id_type=MESH,
        ).wait_recv()
        stage(sender)

    def spread(parts):
        return jnp.concatenate(
            [
                jnp.concatenate(parts[b : b + wave_blocks + 1], axis=1)
                for b in range(lag_blocks)
            ],
            axis=0,
        )

    held = lag_blocks * n
    operands, squares = [], []
    for c in range(NCH):
        parts = [staged[pl.ds(ROWS * b + c, n, stride=ROWS * blocks), :] for b in range(blocks)]
        operands.append(spread([x.astype(jnp.bfloat16) for x in parts]))
        high = [(x * x).astype(jnp.bfloat16) for x in parts]
        low = [(x * x - h.astype(F32)).astype(jnp.bfloat16) for x, h in zip(parts, high)]
        squares.append((spread(high), spread(low)))
    fitted = [None] * own
    for c in range(NCH):
        stacked = jnp.concatenate([operands[c], *squares[c]], axis=0)
        sums = jnp.dot(stacked, window, preferred_element_type=F32)
        mean_one = sums[:held] / L
        mean_two = (sums[held : 2 * held] + sums[2 * held :]) / L
        inverse = 1.0 / jnp.sqrt(mean_two - mean_one * mean_one + 1e-05)
        products = jnp.dot(operands[c], bands[c], preferred_element_type=F32)
        for t in range(own):
            term = products[:, LANES * t : LANES * (t + 1)] * (inverse * factors_ref[c, t : t + 1, :])
            fitted[t] = term if c == 0 else fitted[t] + term

    lane = lax.broadcasted_iota(jnp.int32, (n, LANES), 1)
    for t in range(own):
        code = jnp.broadcast_to(codes[t], (n, LANES))
        shift = code & 127
        member = code >= 256
        turn = (lane + shift) & (LANES - 1)
        current = jnp.take_along_axis(
            fitted[t], jnp.concatenate([turn] * lag_blocks, axis=0), axis=1,
            mode="promise_in_bounds",
        )
        stays = lane + shift < LANES
        for b in range(out_blocks):
            picked = jnp.where(
                stays, current[n * b : n * (b + 1)], current[n * (b + 1) : n * (b + 2)]
            )
            out_ref[t : t + 1, LANES * b : LANES * (b + 1)] = jnp.sum(
                jnp.where(member, picked, 0.0), axis=0, keepdims=True
            )

    @pl.loop(1, n)
    def sent(step):
        copy_to(step).wait_send()


def body(n, data, templates, station_lists, counts, offsets):
    own, _, length = templates.shape
    operands = (data, jnp.transpose(templates, (1, 0, 2)), station_lists, counts[None, :], offsets)
    return pl.pallas_call(
        functools.partial(network_kernel, n),
        out_shape=jax.ShapeDtypeStruct((own, NTAU), F32),
        in_specs=[pl.BlockSpec(memory_space=pltpu.HBM)] * len(operands),
        out_specs=pl.BlockSpec(memory_space=pltpu.VMEM),
        scratch_shapes=[pltpu.VMEM(x.shape, x.dtype) for x in operands[1:]]
        + [
            pltpu.VMEM((n, *data.shape[1:]), data.dtype),
            pltpu.VMEM((n * ROWS * (data.shape[2] // LANES), LANES), F32),
            pltpu.VMEM((NCH, length + LANES, own * LANES), jnp.bfloat16),
            pltpu.VMEM((NCH, own, LANES), F32),
            pltpu.SemaphoreType.DMA((len(operands),)),
            pltpu.SemaphoreType.DMA((n,)),
            pltpu.SemaphoreType.DMA((n,)),
        ],
        compiler_params=pltpu.CompilerParams(
            collective_id=0, has_side_effects=True, vmem_limit_bytes=40 * 1024 * 1024
        ),
    )(*[pltpu.with_memory_space_constraint(x, pltpu.HBM) for x in operands])


def solution(mesh):
    placed = (P(("parts", "sta"), None, None), P("sta", None, None), P(), P(), P())
    return jax.shard_map(
        functools.partial(body, mesh.shape["sta"]), mesh=mesh, in_specs=placed,
        out_specs=P(("parts", "sta"), None), check_vma=False,
    )
```
